32 devices in a mesh: seq: 8 (over z, y), branch: 4 (over x, core).
Axes of the slice: x: 2, y: 2, z: 4, core: 2. Of those that a mesh axis runs over, the one named last changes fastest.
Arguments:
- q_ctl: bfloat16 [4, 1536, 2048], P('branch', 'seq'), may hold values from -64 to 64
- k_ctl: bfloat16 [4, 1536, 2048], P('branch', 'seq'), may hold values from -64 to 64
- v_ctl: bfloat16 [4, 1536, 2048], P('branch', 'seq'), may hold values from -6 to 6
- positions: int32 [1536], P('seq'), may hold values from 0 to 6143
- branch_ids: int32 [4], P('branch'), may hold values from 0 to 63
- cond_scale: float32 [64], replicated, may hold values from 0.25 to 2
- out_weight: bfloat16 [2048, 3072], P('branch', 'seq'), may hold values from -0.125 to 0.125
- frozen: bfloat16 [1536, 3072], P(('seq', 'branch')), may hold values from -2.390625 to 2.390625
- norm_gain: float32 [3072], replicated, may hold values from 0.5 to 1.5
- cotangent: bfloat16 [1536, 3072], P('seq'), may hold values from -6 to 6
Outputs:
- normed: bfloat16 [1536, 3072], P(('seq', 'branch'))
- grad_attn: bfloat16 [4, 1536, 2048], P('branch', 'seq')
The draws below stay inside these ranges and needn't reach their ends.
All inputs are finite; a program needn't handle non-finite values.
Results may differ from the reference program's by a relative error of at most 0.014.
Values may be sent and summed in bfloat16 or wider, within the bound.
A program may use at most 64 MiB of HBM per device.

```python
import math
import jax
import jax.numpy as jnp
from jax import lax

D = 3072
HEADS = 16
HEAD_DIM = 128
CONDS = 4
ADAPTERS = 64
HD = 2048
LEN = 1536
SEQS = 1
TOKENS = 1536


def query_key_pair(key):
    full_shape = (CONDS, TOKENS, HD)
    key_part = jnp.clip(jax.random.normal(jax.random.fold_in(key, 21), full_shape, jnp.float32), -6.0, 6.0)
    query_part = 2.0 * jnp.clip(jax.random.normal(jax.random.fold_in(key, 22), full_shape, jnp.float32), -6.0, 6.0)
    return (query_part, key_part)


def draw_q_ctl(key, part):
    return query_key_pair(key)[0].astype(jnp.bfloat16)


def draw_k_ctl(key, part):
    return query_key_pair(key)[1].astype(jnp.bfloat16)


def set_ends(values, own_key, least, top_value):
    longest = values.shape.index(max(values.shape))
    spots = []
    for shift in (0, 1):
        where = [jax.random.randint(jax.random.fold_in(own_key, axis), (), 0, length) for axis, length in enumerate(values.shape)]
        where[longest] = (where[longest] + shift) % values.shape[longest]
        spots.append(tuple(where))
    return values.at[spots[0]].set(least).at[spots[1]].set(top_value)


def steps_of(own_key, extent, split, low, top_value):
    gain, own = 1.0, jax.random.fold_in(own_key, 6)
    for position, parts in split:
        heights = jnp.exp(jax.random.uniform(jax.random.fold_in(own, position), (parts,), jnp.float32, low / len(split), top_value / len(split)))
        gain = gain * jnp.repeat(heights, extent[position] // parts).reshape([-1 if axis == position else 1 for axis in range(len(extent))])
    return gain


def noise(stream_key, dims, deviation, limit, pieces=(), kind=jnp.bfloat16):
    factor_of = steps_of(stream_key, dims, pieces, -0.22, 0.18) if pieces else 1.0
    entries = jax.random.normal(stream_key, dims, jnp.float32) * deviation * factor_of
    return jnp.minimum(jnp.maximum(entries, -limit), limit).astype(kind)


def setup_inputs(seed: int = 0) -> dict:
    arg_keys = jax.random.split(jax.random.key(seed), 11)
    q_ctl = draw_q_ctl(jax.random.fold_in(arg_keys[10], 71), 0)
    k_ctl = draw_k_ctl(jax.random.fold_in(arg_keys[10], 71), 0)
    v_ctl = noise(arg_keys[2], (CONDS, TOKENS, HD), 1.0, 6.0, ((0, 4), (1, 8)))
    positions = set_ends(jax.random.randint(arg_keys[3], (TOKENS,), 0, 4 * LEN), jax.random.fold_in(arg_keys[3], 1), 0, (4 * LEN) - 1).astype(jnp.int32)
    branch_ids = set_ends(jax.random.randint(arg_keys[4], (CONDS,), 0, ADAPTERS), jax.random.fold_in(arg_keys[4], 1), 0, ADAPTERS - 1).astype(jnp.int32)
    cond_scale = jnp.clip(jnp.exp(jax.random.uniform(arg_keys[5], (ADAPTERS,), jnp.float32, math.log(0.25), math.log(2.0))), 0.25, 2.0)
    out_weight = noise(arg_keys[6], (HD, D), HD ** -0.5, 0.125, ((0, 4), (1, 8)))
    frozen = noise(arg_keys[7], (TOKENS, D), 0.3, 2.390625, ((0, 32),))
    norm_gain = jnp.clip(1.0 + 0.1 * jax.random.normal(arg_keys[8], (D,), jnp.float32), 0.5, 1.5)
    cotangent = noise(arg_keys[9], (TOKENS, D), 1.0, 6.0, ((0, 8),))
    return dict(q_ctl=q_ctl, k_ctl=k_ctl, v_ctl=v_ctl, positions=positions, branch_ids=branch_ids, cond_scale=cond_scale, out_weight=out_weight, frozen=frozen, norm_gain=norm_gain, cotangent=cotangent)


EPS = 1e-06

def rope_tables(positions, head_dim):
    exponents = jnp.arange(head_dim // 2, dtype=jnp.float32) * (2.0 / head_dim)
    frequencies = 10000.0 ** (-exponents)
    angles = positions.astype(jnp.float32)[..., None] * frequencies
    return (jnp.cos(angles), jnp.sin(angles))

def rotate(values_in, cosines, sines):
    half_dim = values_in.shape[-1] // 2
    front_half = values_in[..., :half_dim]
    back_half = values_in[..., half_dim:]
    return jnp.concatenate([front_half * cosines - back_half * sines, back_half * cosines + front_half * sines], axis=-1)

def normalize(hidden, norm_gain):
    inverse = lax.rsqrt(lax.optimization_barrier(jnp.mean(hidden * hidden, axis=-1, keepdims=True)) + EPS)
    return (hidden * inverse * norm_gain).astype(jnp.bfloat16)

def norm_grad(hidden, norm_gain, cotangent):
    inverse = lax.rsqrt(lax.optimization_barrier(jnp.mean(hidden * hidden, axis=-1, keepdims=True)) + EPS)
    upstream = cotangent.astype(jnp.float32) * norm_gain
    inner_mean = lax.optimization_barrier(jnp.mean(upstream * hidden, axis=-1, keepdims=True))
    return (inverse * upstream - hidden * (inverse * inverse * inverse) * inner_mean).astype(jnp.bfloat16)

def attend_one(one_item):
    query_rows, key_rows, value_rows = one_item
    scores = jnp.dot(query_rows, key_rows.T, preferred_element_type=jnp.float32) * (1.0 / math.sqrt(query_rows.shape[-1]))
    row_max = lax.optimization_barrier(jnp.max(scores, axis=-1, keepdims=True))
    weights = jnp.exp(scores - row_max)
    row_total = lax.optimization_barrier(jnp.sum(weights, axis=-1, keepdims=True))
    weights_low = (weights / row_total).astype(jnp.bfloat16)
    return jnp.dot(weights_low, value_rows, preferred_element_type=jnp.float32).astype(jnp.bfloat16)

def reference(q_ctl, k_ctl, v_ctl, positions, branch_ids, cond_scale, out_weight, frozen, norm_gain, cotangent):
    cosines, sines = rope_tables(positions, HEAD_DIM)
    cosines = cosines[None, :, None, :]
    sines = sines[None, :, None, :]

    def rotated(source):
        split_heads = source.astype(jnp.float32).reshape(CONDS, TOKENS, HEADS, HEAD_DIM)
        return rotate(split_heads, cosines, sines).astype(jnp.bfloat16)

    def as_items(split_heads):
        grouped = split_heads.reshape(CONDS, SEQS, LEN, HEADS, HEAD_DIM)
        return jnp.transpose(grouped, (0, 1, 3, 2, 4)).reshape(CONDS * SEQS * HEADS, LEN, HEAD_DIM)
    query_items = as_items(rotated(q_ctl))
    key_items = as_items(rotated(k_ctl))
    value_items = as_items(v_ctl.reshape(CONDS, TOKENS, HEADS, HEAD_DIM))
    outputs = lax.map(attend_one, (query_items, key_items, value_items))
    attended = jnp.transpose(outputs.reshape(CONDS, SEQS, HEADS, LEN, HEAD_DIM), (0, 1, 3, 2, 4)).reshape(CONDS, TOKENS, HD)
    branch_scale = cond_scale[branch_ids]

    def accumulate(carry, pair):
        scale_one, attended_one = pair
        return (carry + scale_one * jnp.dot(attended_one, out_weight, preferred_element_type=jnp.float32), None)
    start_stream = frozen.astype(jnp.float32)
    hidden, unused = lax.scan(accumulate, start_stream, (branch_scale, attended))
    normed = normalize(hidden, norm_gain)
    grad_hidden = norm_grad(hidden, norm_gain, cotangent)
    cot_attn = jnp.dot(grad_hidden, out_weight.T, preferred_element_type=jnp.float32).astype(jnp.bfloat16)
    grad_attn = (branch_scale[:, None, None] * cot_attn.astype(jnp.float32)[None]).astype(jnp.bfloat16)
    return (normed, grad_attn)
```

```python
import functools
import math

import jax
import jax.numpy as jnp
from jax import lax
from jax.experimental import pallas as pl
from jax.experimental.pallas import tpu as pltpu
from jax.sharding import PartitionSpec as P

HEADS = 16
HEAD_DIM = 128
EPS = 1e-06
MESH = pl.DeviceIdType.MESH
F32 = jnp.float32
BF16 = jnp.bfloat16


def remote(src, dst, send_sem, recv_sem, target):
    return pltpu.make_async_remote_copy(
        src_ref=src, dst_ref=dst, send_sem=send_sem, recv_sem=recv_sem,
        device_id=target, device_id_type=MESH,
    )


def aligned(index, size):
    return pl.ds(pl.multiple_of(index * size, size), size)


def attend_kernel(
    group, nb, q_ref, k_ref, v_ref, cos_ref, sin_ref, scale_ref, out_ref,
    qs, ks, qr, kr, vr, obuf, osum, msend, mrow, mcol,
    s_in, r_in, s_sum, r_sum, s_back, r_back, s_turn, r_turn,
):
    c = lax.axis_index("branch")
    seq = lax.axis_index("seq")
    i = lax.rem(seq, group)
    base = seq - i
    rows = q_ref.shape[0]
    part = rows // nb
    hd = HEAD_DIM
    hh = qr.shape[0]
    clip = qr.shape[1]
    width = mcol.shape[1]
    order = list(range(group - 1, 0, -1))

    def seq_peer(d):
        return base + jnp.bitwise_xor(i, d)

    def branch_peer(d):
        return jnp.bitwise_xor(c, d)

    barrier = pltpu.get_barrier_semaphore()
    for d in order:
        pl.semaphore_signal(barrier, inc=1, device_id={"seq": seq_peer(d)}, device_id_type=MESH)
    for d in range(1, nb):
        pl.semaphore_signal(barrier, inc=1, device_id={"branch": branch_peer(d)}, device_id_type=MESH)
    pl.semaphore_wait(barrier, group - 1 + nb - 1)

    cosines = cos_ref[...]
    sines = sin_ref[...]

    def rotate(src, cols):
        x = src[:, cols].astype(F32)
        return (x * cosines + pltpu.roll(x, hd // 2, 1) * sines).astype(BF16)

    mine = aligned(i, rows)
    sends = []
    arrivals = [[] for _ in range(hh)]

    def send_in(kind, h, d, src, dst):
        copy = remote(src, dst, s_in.at[kind, h, d], r_in.at[kind, h, d], {"seq": seq_peer(d)})
        copy.start()
        sends.append(copy)
        arrivals[h].append(copy)

    for h in range(hh):
        for d in order:
            cols = aligned(jnp.bitwise_xor(i, d) * hh + h, hd)
            send_in(2, h, d, v_ref.at[:, cols], vr.at[h, mine, :])
            ks[:, cols] = rotate(k_ref, cols)
            send_in(1, h, d, ks.at[:, cols], kr.at[h, mine, :])
            qs[:, cols] = rotate(q_ref, cols)
            send_in(0, h, d, qs.at[:, cols], qr.at[h, mine, :])
        cols = aligned(i * hh + h, hd)
        vr[h, mine, :] = v_ref[:, cols]
        kr[h, mine, :] = rotate(k_ref, cols)
        qr[h, mine, :] = rotate(q_ref, cols)

    factor = (1.0 / math.sqrt(hd)) * math.log2(math.e)
    scale = scale_ref[0, 0]
    block = rows
    sums = [[] for _ in range(hh)]
    for h in range(hh):
        for copy in arrivals[h]:
            copy.wait_recv()

        def one_block(n, carry, h=h):
            q = qr[h, aligned(n, block), :]
            s = lax.dot_general(q, kr[h], (((1,), (1,)), ((), ())), preferred_element_type=F32)
            top = jnp.max(s, axis=-1, keepdims=True)
            p = jnp.exp2((s - top) * factor)
            total = jnp.sum(p, axis=-1, keepdims=True)
            o = jnp.dot(p.astype(BF16), vr[h], preferred_element_type=F32)
            obuf[h, n] = (o * (scale / total)).astype(BF16)
            return carry

        lax.fori_loop(0, clip // block, one_block, 0)
        for d in range(nb - 1, 0, -1):
            copy = remote(
                obuf.at[h, :, aligned(branch_peer(d), part), :], osum.at[h, d - 1],
                s_sum.at[h, d], r_sum.at[h, d], {"branch": branch_peer(d)},
            )
            copy.start()
            sends.append(copy)
            sums[h].append(copy)

    backs = []
    for h in range(hh):
        for copy in sums[h]:
            copy.wait_recv()
        total = obuf[h, :, aligned(c, part), :].astype(F32)
        for d in range(1, nb):
            total = total + osum[h, d - 1].astype(F32)
        msend[h] = total.astype(BF16)
        cols = aligned(i * hh + h, hd)
        for d in order:
            copy = remote(
                msend.at[h, jnp.bitwise_xor(i, d)], mrow.at[:, cols],
                s_back.at[h, d], r_back.at[h, d], {"seq": seq_peer(d)},
            )
            copy.start()
            sends.append(copy)
            backs.append(copy)
        mrow[:, cols] = msend[h, i]
    for copy in backs:
        copy.wait_recv()

    turns = []
    for d in range(nb - 1, 0, -1):
        copy = remote(
            mrow.at[:, aligned(branch_peer(d), width)], mcol.at[aligned(c, part), :],
            s_turn.at[d], r_turn.at[d], {"branch": branch_peer(d)},
        )
        copy.start()
        sends.append(copy)
        turns.append(copy)
    mcol[aligned(c, part), :] = mrow[:, aligned(c, width)]
    for copy in turns:
        copy.wait_recv()
    out_ref[...] = mcol[...]
    for copy in sends:
        copy.wait_send()


def norm_kernel(
    chunks, m_ref, w_ref, frozen_ref, gain_ref, cot_ref, scale_ref, normed_ref, grad_ref,
    part, ra, sx, rx, hid, gh, cb,
    s_a, r_a, s_x, r_x, s_g, r_g, s_c, r_c,
):
    c = lax.axis_index("branch")
    near = jnp.bitwise_xor(c, 1)
    far = jnp.bitwise_xor(c, 2)
    across = jnp.bitwise_xor(c, 3)
    to_near = {"branch": near}
    to_far = {"branch": far}
    rows = m_ref.shape[0]
    quarter = frozen_ref.shape[0]
    depth, model = w_ref.shape
    step = model // chunks
    spans = [pl.ds(n * step, step) for n in range(chunks)]

    barrier = pltpu.get_barrier_semaphore()
    for target in (to_near, to_far):
        pl.semaphore_signal(barrier, inc=1, device_id=target, device_id_type=MESH)
    pl.semaphore_wait(barrier, 2)

    sends = []

    def send(src, dst, send_sem, recv_sem, target):
        copy = remote(src, dst, send_sem, recv_sem, target)
        copy.start()
        sends.append(copy)
        return copy

    first = []
    for n, span in enumerate(spans):
        part[:, span] = jnp.dot(
            m_ref[...], w_ref[:, span], preferred_element_type=F32
        ).astype(BF16)
        a = send(part.at[aligned(across, quarter), span], ra.at[1, :, span], s_a.at[1, n], r_a.at[1, n], to_near)
        b = send(part.at[aligned(near, quarter), span], ra.at[0, :, span], s_a.at[0, n], r_a.at[0, n], to_near)
        first.append((b, a))
    second = []
    for n, span in enumerate(spans):
        first[n][1].wait_recv()
        sx[:, span] = (
            part[aligned(far, quarter), span].astype(F32) + ra[1, :, span].astype(F32)
        ).astype(BF16)
        second.append(send(sx.at[:, span], rx.at[:, span], s_x.at[n], r_x.at[n], to_far))
    for n, span in enumerate(spans):
        first[n][0].wait_recv()
        hid[:, span] = (
            part[aligned(c, quarter), span].astype(F32)
            + ra[0, :, span].astype(F32)
            + frozen_ref[:, span].astype(F32)
        )
    square = jnp.zeros((quarter, 1), F32)
    inner = jnp.zeros((quarter, 1), F32)
    for n, span in enumerate(spans):
        second[n].wait_recv()
        value = hid[:, span] + rx[:, span].astype(F32)
        hid[:, span] = value
        up = cot_ref[aligned(c, quarter), span].astype(F32) * gain_ref[:, span]
        square = square + jnp.sum(value * value, axis=-1, keepdims=True)
        inner = inner + jnp.sum(up * value, axis=-1, keepdims=True)
    r = lax.rsqrt(square * (1.0 / model) + EPS)
    bend = r * r * r * (inner * (1.0 / model))
    own_far, own_near = [], []
    for n, span in enumerate(spans):
        up = cot_ref[aligned(c, quarter), span].astype(F32) * gain_ref[:, span]
        mine = gh.at[aligned(c, quarter), span]
        gh[aligned(c, quarter), span] = (r * up - hid[:, span] * bend).astype(BF16)
        own_far.append(send(mine, mine, s_g.at[0, n], r_g.at[0, n], to_far))
        own_near.append(send(mine, mine, s_g.at[1, n], r_g.at[1, n], to_near))
    for span in spans:
        normed_ref[:, span] = (hid[:, span] * r * gain_ref[:, span]).astype(BF16)
    passed = []
    for n, span in enumerate(spans):
        own_far[n].wait_recv()
        block = gh.at[aligned(far, quarter), span]
        passed.append(send(block, block, s_g.at[2, n], r_g.at[2, n], to_near))
    total = jnp.zeros((rows, depth), F32)
    for n, span in enumerate(spans):
        own_near[n].wait_recv()
        passed[n].wait_recv()
        total = total + lax.dot_general(
            gh[:, span], w_ref[:, span], (((1,), (1,)), ((), ())), preferred_element_type=F32
        )
    cb[c] = total.astype(BF16)
    out_far = send(cb.at[c], cb.at[c], s_c.at[0], r_c.at[0], to_far)
    out_near = send(cb.at[c], cb.at[c], s_c.at[1], r_c.at[1], to_near)
    scale = scale_ref[0, 0]

    def put(index):
        grad_ref[:, aligned(index, depth)] = (scale * cb[index].astype(F32)).astype(BF16)

    put(c)
    out_near.wait_recv()
    put(near)
    out_far.wait_recv()
    out_pass = send(cb.at[far], cb.at[far], s_c.at[2], r_c.at[2], to_near)
    put(far)
    out_pass.wait_recv()
    put(across)
    for copy in sends:
        copy.wait_send()


def on_device(
    q_ctl, k_ctl, v_ctl, positions, branch_ids, cond_scale, out_weight, frozen, norm_gain, cotangent
):
    nb = lax.axis_size("branch")
    group = min(HEADS, lax.axis_size("seq"))
    rows, features = q_ctl.shape[1:]
    hh = HEADS // group
    clip = group * rows
    part = rows // nb
    model = cotangent.shape[1]
    depth = features // nb
    hd = HEAD_DIM
    exponents = jnp.arange(hd // 2, dtype=F32) * (2.0 / hd)
    frequencies = 10000.0 ** (-exponents)
    angles = positions.astype(F32)[:, None] * frequencies
    cosines, sines = jnp.cos(angles), jnp.sin(angles)
    cosines = jnp.concatenate([cosines, cosines], axis=-1)
    sines = jnp.concatenate([-sines, sines], axis=-1)
    scale = jnp.sum(
        jnp.where(jnp.arange(cond_scale.shape[0]) == branch_ids[0], cond_scale, 0.0)
    ).reshape(1, 1)
    weight = lax.all_gather(out_weight, "seq", axis=1, tiled=True)
    vmem = pl.BlockSpec(memory_space=pltpu.VMEM)
    smem = pl.BlockSpec(memory_space=pltpu.SMEM)
    dma = pltpu.SemaphoreType.DMA
    mixed = pl.pallas_call(
        functools.partial(attend_kernel, group, nb),
        out_shape=jax.ShapeDtypeStruct((rows, depth), BF16),
        in_specs=[vmem] * 5 + [smem],
        out_specs=vmem,
        scratch_shapes=[
            pltpu.VMEM((rows, features), BF16),
            pltpu.VMEM((rows, features), BF16),
            pltpu.VMEM((hh, clip, hd), BF16),
            pltpu.VMEM((hh, clip, hd), BF16),
            pltpu.VMEM((hh, clip, hd), BF16),
            pltpu.VMEM((hh, group, rows, hd), BF16),
            pltpu.VMEM((hh, nb - 1, group, part, hd), BF16),
            pltpu.VMEM((hh, group, part, hd), BF16),
            pltpu.VMEM((part, features), BF16),
            pltpu.VMEM((rows, depth), BF16),
            dma((3, hh, group)), dma((3, hh, group)),
            dma((hh, nb)), dma((hh, nb)),
            dma((hh, group)), dma((hh, group)),
            dma((nb,)), dma((nb,)),
        ],
        compiler_params=pltpu.CompilerParams(
            collective_id=0, has_side_effects=True, vmem_limit_bytes=40 << 20
        ),
        cost_estimate=pl.CostEstimate(
            flops=4 * hh * clip * clip * hd, bytes_accessed=6 * rows * features,
            transcendentals=hh * clip * clip,
        ),
        name="attend",
    )(q_ctl[0], k_ctl[0], v_ctl[0], cosines, sines, scale)
    chunks = 4 if model % (4 * 128) == 0 else 1
    normed, grad = pl.pallas_call(
        functools.partial(norm_kernel, chunks),
        out_shape=(
            jax.ShapeDtypeStruct((part, model), BF16),
            jax.ShapeDtypeStruct((rows, features), BF16),
        ),
        in_specs=[vmem] * 5 + [smem],
        out_specs=(vmem, vmem),
        scratch_shapes=[
            pltpu.VMEM((rows, model), BF16),
            pltpu.VMEM((2, part, model), BF16),
            pltpu.VMEM((part, model), BF16),
            pltpu.VMEM((part, model), BF16),
            pltpu.VMEM((part, model), F32),
            pltpu.VMEM((rows, model), BF16),
            pltpu.VMEM((nb, rows, depth), BF16),
            dma((2, chunks)), dma((2, chunks)),
            dma((chunks,)), dma((chunks,)),
            dma((3, chunks)), dma((3, chunks)),
            dma((3,)), dma((3,)),
        ],
        compiler_params=pltpu.CompilerParams(
            collective_id=1, has_side_effects=True, vmem_limit_bytes=40 << 20
        ),
        cost_estimate=pl.CostEstimate(
            flops=4 * rows * model * depth, bytes_accessed=2 * model * depth, transcendentals=0
        ),
        name="inject",
    )(mixed, weight, frozen, norm_gain.reshape(1, model), cotangent, scale)
    return (normed, grad.reshape(1, rows, features))


def solution(mesh):
    return jax.shard_map(
        on_device,
        mesh=mesh,
        in_specs=(
            P("branch", "seq", None),
            P("branch", "seq", None),
            P("branch", "seq", None),
            P("seq"),
            P("branch"),
            P(),
            P("branch", "seq"),
            P(("seq", "branch"), None),
            P(),
            P("seq", None),
        ),
        out_specs=(P(("seq", "branch"), None), P("branch", "seq", None)),
        check_vma=False,
    )
```
